32 devices in a mesh: dp: 2 (over x), seq: 4 (over z), fsdp: 4 (over y, core).
Axes of the slice: x: 2, y: 2, z: 4, core: 2. Of those that a mesh axis runs over, the one named last changes fastest.
Arguments:
- tokens: bfloat16 [2, 8, 2048, 768], P(None, ('dp', 'fsdp'), 'seq'), may hold values from -6 to 6
- lengths: int32 [2, 8], replicated, may hold values from 1 to 2048, as said below
- in_weight: bfloat16 [768, 2304], P(('dp', 'seq'), 'fsdp'), may hold values from -0.21875 to 0.21875
- in_bias: bfloat16 [1536], P(('dp', 'seq')), may hold values from -3 to 3
- out_weight: bfloat16 [768, 768], P(('dp', 'seq'), 'fsdp'), may hold values from -6 to 6
- out_bias: bfloat16 [768], P(('dp', 'seq')), may hold values from -3 to 3
- mid_gain: bfloat16 [768], P(('dp', 'seq')), may hold values from 0.099609375 to 1.8984375
- mid_shift: bfloat16 [768], P(('dp', 'seq')), may hold values from -3 to 3
- up_weight: bfloat16 [768, 3072], P(('dp', 'seq'), 'fsdp'), may hold values from -0.21875 to 0.21875
- up_bias: bfloat16 [3072], P(('dp', 'seq')), may hold values from -3 to 3
- down_weight: bfloat16 [3072, 768], P(('dp', 'seq'), 'fsdp'), may hold values from -0.109375 to 0.109375
- down_bias: bfloat16 [768], P(('dp', 'seq')), may hold values from -3 to 3
- last_gain: bfloat16 [768], P(('dp', 'seq')), may hold values from 0.099609375 to 1.8984375
- last_shift: bfloat16 [768], P(('dp', 'seq')), may hold values from -3 to 3
- grad_output: bfloat16 [2, 8, 2048, 768], P(None, ('dp', 'fsdp'), 'seq'), may hold values from -6 to 6
Outputs:
- output: bfloat16 [2, 8, 2048, 768], P(None, ('dp', 'fsdp'), 'seq')
- grad_tokens: float32 [2, 8, 2048, 768], P(None, ('dp', 'fsdp'), 'seq')
- grad_in_weight: float32 [768, 2304], P(('dp', 'seq'), 'fsdp')
- grad_in_bias: float32 [1536], P(('dp', 'seq'))
- grad_out_weight: float32 [768, 768], P(('dp', 'seq'), 'fsdp')
- grad_out_bias: float32 [768], P(('dp', 'seq'))
- grad_mid_gain: float32 [768], P(('dp', 'seq'))
- grad_mid_shift: float32 [768], P(('dp', 'seq'))
- grad_up_weight: float32 [768, 3072], P(('dp', 'seq'), 'fsdp')
- grad_up_bias: float32 [3072], P(('dp', 'seq'))
- grad_down_weight: float32 [3072, 768], P(('dp', 'seq'), 'fsdp')
- grad_down_bias: float32 [768], P(('dp', 'seq'))
- grad_last_gain: float32 [768], P(('dp', 'seq'))
- grad_last_shift: float32 [768], P(('dp', 'seq'))
The draws below stay inside these ranges and needn't reach their ends.
Inputs may be any that keep to these rules, and one draw needn't show every extreme that they name: lengths[m, b] counts the valid tokens of sequence b of micro-batch m, the first ones; the rest is padding. Of the 2 sequences b = j * 1 to (j + 1) - 1 of all micro-batches, at least one has length 2048.
All inputs are finite; a program needn't handle non-finite values.
Results may differ from the reference program's by a relative error of at most 0.02.
Values may be sent and summed in bfloat16 or wider, within the bound.
No kernel may reach another device: no remote copies, remote signals or barrier semaphores. Data moves between devices by JAX's collectives and lax.ppermute only.
A program may use at most 384 MiB of HBM per device.

```python
import math
import jax
import jax.numpy as jnp
from jax import lax

D = 768
HEADS = 12
HEAD = 64
FF = 3072
S_DP = 1
MICRO = 2
LEN = 2048
SEQS = 8


def draw_lengths(key, part):
    first, second = jax.random.split(key)
    base = jax.random.randint(first, (MICRO, SEQS), 1, LEN + 1)
    groups = SEQS // S_DP
    chosen = jax.random.randint(second, (groups,), 0, MICRO * S_DP)
    column = jnp.arange(SEQS, dtype=jnp.int32)
    micro_index = jnp.arange(MICRO, dtype=jnp.int32)
    slot = micro_index[:, None] * S_DP + (column % S_DP)[None, :]
    full = slot == chosen[column // S_DP][None, :]
    return jnp.where(full, LEN, base).astype(jnp.int32)


def shard_levels(key, extent, pieces, low, top_value):
    level, own = 1.0, jax.random.fold_in(key, 6)
    for dim, parts in pieces:
        steps = jnp.exp(jax.random.uniform(jax.random.fold_in(own, dim), (parts,), jnp.float32, low / len(pieces), top_value / len(pieces)))
        level = level * jnp.repeat(steps, extent[dim] // parts).reshape([-1 if axis == dim else 1 for axis in range(len(extent))])
    return level


def noise(own_key, shape, spread, most, shards=(), kind=jnp.bfloat16):
    values = spread * jax.random.normal(own_key, shape, jnp.float32)
    if shards:
        values = values * shard_levels(own_key, shape, shards, -0.22, 0.18)
    return jnp.clip(values, -most, most).astype(kind)


def setup_inputs(seed: int = 0) -> dict:
    key_list = jax.random.split(jax.random.key(seed), 16)
    tokens = noise(key_list[0], (MICRO, SEQS, LEN, D), 1.0, 6.0, ((1, 8), (2, 4)))
    lengths = draw_lengths(jax.random.fold_in(key_list[15], 71), 0)
    in_weight = noise(key_list[2], (D, 3 * D), D ** -0.5, 0.21875, ((0, 8), (1, 4)))
    in_bias = noise(key_list[3], (2 * D,), 0.5, 3.0, ((0, 8),))
    out_weight = noise(key_list[4], (D, D), 1 ** -0.5, 6.0, ((0, 8), (1, 4)))
    out_bias = noise(key_list[5], (D,), 0.5, 3.0, ((0, 8),))
    mid_gain = jnp.clip(1.0 + 0.18 * jax.random.normal(key_list[6], (D,), jnp.float32), 0.099609375, 1.8984375).astype(jnp.bfloat16)
    mid_shift = noise(key_list[7], (D,), 0.5, 3.0, ((0, 8),))
    up_weight = noise(key_list[8], (D, FF), D ** -0.5, 0.21875, ((0, 8), (1, 4)))
    up_bias = noise(key_list[9], (FF,), 0.5, 3.0, ((0, 8),))
    down_weight = noise(key_list[10], (FF, D), FF ** -0.5, 0.109375, ((0, 8), (1, 4)))
    down_bias = noise(key_list[11], (D,), 0.5, 3.0, ((0, 8),))
    last_gain = jnp.clip(1.0 + 0.18 * jax.random.normal(key_list[12], (D,), jnp.float32), 0.099609375, 1.8984375).astype(jnp.bfloat16)
    last_shift = noise(key_list[13], (D,), 0.5, 3.0, ((0, 8),))
    grad_output = noise(key_list[14], (MICRO, SEQS, LEN, D), 1.0, 6.0, ((1, 8), (2, 4)))
    return dict(tokens=tokens, lengths=lengths, in_weight=in_weight, in_bias=in_bias, out_weight=out_weight, out_bias=out_bias, mid_gain=mid_gain, mid_shift=mid_shift, up_weight=up_weight, up_bias=up_bias, down_weight=down_weight, down_bias=down_bias, last_gain=last_gain, last_shift=last_shift, grad_output=grad_output)


epsilon = 1e-05
highest = lax.Precision.HIGHEST

@jax.custom_vjp
def low(v):
    return lax.optimization_barrier(v.astype(jnp.bfloat16)).astype(jnp.float32)

@jax.custom_vjp
def low_back(v):
    return v

def low_keep(v):
    return (low(v), None)

def low_pass(kept, grad):
    return (grad,)

def back_keep(v):
    return (v, None)

def back_low(kept, grad):
    return (low(grad),)
low.defvjp(low_keep, low_pass)
low_back.defvjp(back_keep, back_low)

def layer_norm(hidden, gain, shift):
    centered = hidden - lax.optimization_barrier(jnp.mean(hidden, axis=-1, keepdims=True))
    scale = lax.rsqrt(lax.optimization_barrier(jnp.mean(centered * centered, axis=-1, keepdims=True)) + epsilon)
    return centered * scale * gain + shift

def attention(queries, keys, values, length):
    span = queries.shape[0]
    block = min(512, span)
    valid = jnp.arange(span, dtype=jnp.int32) < length

    def one_block(query_block):
        scores = jnp.einsum('qhd,khd->hqk', query_block, keys, precision=highest) * (1.0 / math.sqrt(HEAD))
        scores = low_back(scores)
        scores = jnp.where(valid[None, None, :], scores, -jnp.inf)
        top = lax.optimization_barrier(jnp.max(scores, axis=-1, keepdims=True))
        weights = jnp.exp(scores - top)
        probs = low(weights / lax.optimization_barrier(jnp.sum(weights, axis=-1, keepdims=True)))
        return jnp.einsum('hqk,khd->qhd', probs, values, precision=highest)
    blocks = lax.map(jax.checkpoint(one_block), queries.reshape(span // block, block, HEADS, HEAD))
    return blocks.reshape(span, HEADS * HEAD)

def forward_seq(seq_tokens, length, in_weight, in_bias, out_weight, out_bias, mid_gain, mid_shift, up_weight, up_bias, down_weight, down_bias, last_gain, last_shift):
    span = seq_tokens.shape[0]
    paired = in_bias.reshape(HEADS, 2, HEAD)
    full_bias = jnp.stack([paired[:, 0], jnp.zeros_like(paired[:, 0]), paired[:, 1]], axis=1).reshape(3 * D)
    proj = jnp.dot(seq_tokens, in_weight, precision=highest) + full_bias
    proj = low(low_back(proj)).reshape(span, HEADS, 3, HEAD)
    attended = attention(proj[:, :, 0], proj[:, :, 1], proj[:, :, 2], length)
    attended = low(low_back(attended))
    mixed = low_back(jnp.dot(attended, out_weight, precision=highest) + out_bias)
    normed = layer_norm(seq_tokens + mixed, mid_gain, mid_shift)
    pre_up = low_back(jnp.dot(low(normed), up_weight, precision=highest) + up_bias)
    act = low(jax.nn.gelu(pre_up, approximate=False))
    branch = low_back(jnp.dot(act, down_weight, precision=highest) + down_bias)
    return layer_norm(normed + branch, last_gain, last_shift)

def reference(tokens, lengths, in_weight, in_bias, out_weight, out_bias, mid_gain, mid_shift, up_weight, up_bias, down_weight, down_bias, last_gain, last_shift, grad_output):
    params = tuple((weight.astype(jnp.float32) for weight in (in_weight, in_bias, out_weight, out_bias, mid_gain, mid_shift, up_weight, up_bias, down_weight, down_bias, last_gain, last_shift)))
    all_tokens = tokens.reshape(MICRO * SEQS, LEN, D)
    all_grads = grad_output.reshape(MICRO * SEQS, LEN, D)
    all_lengths = lengths.reshape(MICRO * SEQS)

    def one_seq(totals, item):
        seq_tokens, seq_grad, length = item

        def run(seq_float, *weights):
            return forward_seq(seq_float, length, *weights)
        result, pullback = jax.vjp(run, seq_tokens.astype(jnp.float32), *params)
        grads = pullback(seq_grad.astype(jnp.float32))
        totals = tuple((total + grad for total, grad in zip(totals, grads[1:])))
        return (totals, (result.astype(jnp.bfloat16), grads[0]))
    start = tuple((jnp.zeros_like(weight) for weight in params))
    totals, (results, grad_seq) = lax.scan(one_seq, start, (all_tokens, all_grads, all_lengths))
    return (results.reshape(MICRO, SEQS, LEN, D), grad_seq.reshape(MICRO, SEQS, LEN, D), totals[0], totals[1], totals[2], totals[3], totals[4], totals[5], totals[6], totals[7], totals[8], totals[9], totals[10], totals[11])
```

```python
import math
import jax
import jax.numpy as jnp
from jax import lax
from jax.experimental import pallas as pl
from jax.experimental.pallas import tpu as pltpu
from jax.sharding import PartitionSpec as P

D = 768
HEADS = 12
HEAD = 64
FF = 3072
MICRO = 2
LOG2E = math.log2(math.e)
NT = (((1,), (1,)), ((), ()))
TN = (((0,), (0,)), ((), ()))
f32 = jnp.float32
bf16 = jnp.bfloat16


def dot(a, b, dims=(((1,), (0,)), ((), ()))):
    return lax.dot_general(a, b, dims, preferred_element_type=f32)


def lane_of(shape):
    return lax.broadcasted_iota(jnp.int32, shape, 1)


def attend_kernel(q_ref, k_ref, v_ref, o_ref, qa_ref):
    rows = q_ref.shape[1]
    lane = lane_of((rows, 128))
    halves = []
    for h in range(2):
        q = q_ref[h]
        s = dot(q, k_ref[h], NT)
        top = jnp.max(s, axis=-1, keepdims=True)
        p = jnp.exp2(s - top).astype(bf16)
        o = dot(p, v_ref[h])
        total = -o[:, 64:65]
        halves.append(o / total)
        level = top + jnp.log2(total)
        high = level.astype(bf16)
        rest = level - high.astype(f32)
        mid = rest.astype(bf16)
        low = (rest - mid.astype(f32)).astype(bf16)
        qa_ref[h] = jnp.where(
            lane < 65,
            q.astype(f32),
            jnp.where(
                lane == 65,
                high.astype(f32),
                jnp.where(lane == 66, mid.astype(f32), jnp.where(lane == 67, low.astype(f32), 0.0)),
            ),
        ).astype(bf16)
    o_ref[...] = jnp.where(lane < 64, halves[0], pltpu.roll(halves[1], 64, 1)).astype(bf16)


def attend(q, k, v, block=512):
    n, span, _ = q.shape
    whole = pl.BlockSpec((2, span, 128), lambda p, i: (p, 0, 0))
    part = pl.BlockSpec((2, block, 128), lambda p, i: (p, i, 0))
    return pl.pallas_call(
        attend_kernel,
        grid=(n // 2, span // block),
        in_specs=[part, whole, whole],
        out_specs=[pl.BlockSpec((block, 128), lambda p, i: (i, p)), part],
        out_shape=[
            jax.ShapeDtypeStruct((span, n * 64), bf16),
            jax.ShapeDtypeStruct((n, span, 128), bf16),
        ],
        compiler_params=pltpu.CompilerParams(vmem_limit_bytes=56 * 2**20),
        cost_estimate=pl.CostEstimate(
            flops=n * span * span * 512, bytes_accessed=n * span * 1024, transcendentals=n * span * span
        ),
        name="attend",
    )(q, k, v)


def attend_back_kernel(q_ref, k_ref, v_ref, o_ref, g_ref, dq_ref, dk_ref, dv_ref, ga_ref, acc_ref):
    step = pl.program_id(1)
    span = q_ref.shape[1]
    rows = k_ref.shape[1]

    @pl.when(step == 0)
    def _():
        lane = lane_of((span, 128))
        grad = g_ref[...].astype(f32)
        prod = grad * o_ref[...].astype(f32)
        for h in range(2):
            mine = (lane < 64) if h == 0 else (lane >= 64)
            delta = jnp.sum(jnp.where(mine, prod, 0.0), axis=-1, keepdims=True)
            high = delta.astype(bf16).astype(f32)
            mid = delta - high
            g = grad if h == 0 else pltpu.roll(grad, 64, 1)
            ga_ref[h] = jnp.where(
                lane < 64, g, jnp.where(lane == 64, high, jnp.where(lane == 65, mid, 0.0))
            ).astype(bf16)
        acc_ref[...] = jnp.zeros_like(acc_ref)

    lane = lane_of((rows, 128))
    dks, dvs = [], []
    for h in range(2):
        q = q_ref[h]
        k = k_ref[h]
        g = ga_ref[h]
        p = jnp.exp2(dot(k, q, NT))
        ds = (p * dot(v_ref[h], g, NT)).astype(bf16)
        dvs.append(dot(p.astype(bf16), g))
        dks.append(dot(ds, q))
        acc_ref[h] += dot(ds, k, TN)
    dk_ref[...] = (jnp.where(lane < 64, dks[0], pltpu.roll(dks[1], 64, 1)) * (1.0 / LOG2E)).astype(bf16)
    dv_ref[...] = jnp.where(lane < 64, dvs[0], pltpu.roll(dvs[1], 64, 1)).astype(bf16)

    @pl.when(step == pl.num_programs(1) - 1)
    def _():
        wide = lane_of((span, 128))
        dq_ref[...] = (jnp.where(wide < 64, acc_ref[0], pltpu.roll(acc_ref[1], 64, 1)) * 0.125).astype(bf16)


def attend_back(q, k, v, o, g, block=256):
    n, span, _ = q.shape
    whole = pl.BlockSpec((2, span, 128), lambda p, i: (p, 0, 0))
    part = pl.BlockSpec((2, block, 128), lambda p, i: (p, i, 0))
    flat = pl.BlockSpec((span, 128), lambda p, i: (0, p))
    rows = pl.BlockSpec((block, 128), lambda p, i: (i, p))
    return pl.pallas_call(
        attend_back_kernel,
        grid=(n // 2, span // block),
        in_specs=[whole, part, part, flat, flat],
        out_specs=[flat, rows, rows],
        out_shape=[jax.ShapeDtypeStruct((span, n * 64), bf16)] * 3,
        scratch_shapes=[pltpu.VMEM((2, span, 128), bf16), pltpu.VMEM((2, span, 128), f32)],
        compiler_params=pltpu.CompilerParams(vmem_limit_bytes=56 * 2**20),
        cost_estimate=pl.CostEstimate(
            flops=n * span * span * 1280, bytes_accessed=n * span * 1024, transcendentals=n * span * span
        ),
        name="attend_back",
    )(q, k, v, o, g)


epsilon = 1e-05


def standardize(hidden):
    centered = hidden - jnp.mean(hidden, axis=-1, keepdims=True)
    scale = lax.rsqrt(jnp.mean(centered * centered, axis=-1, keepdims=True) + epsilon)
    return (centered * scale, scale)


def norm_back(grad_out, standard, scale, gain):
    spread = grad_out * gain
    return scale * (
        spread
        - jnp.mean(spread, axis=-1, keepdims=True)
        - standard * jnp.mean(spread * standard, axis=-1, keepdims=True)
    )


def gelu_slope(value):
    return 0.5 * (1.0 + lax.erf(value * (1.0 / math.sqrt(2.0)))) + value * jnp.exp(
        -0.5 * value * value
    ) * (1.0 / math.sqrt(2.0 * math.pi))


def with_key_zeros(query_value):
    paired = query_value.astype(jnp.float32).reshape(HEADS, 2, HEAD)
    return jnp.stack([paired[:, 0], jnp.zeros_like(paired[:, 0]), paired[:, 1]], axis=1).reshape(
        3 * D
    )


def gather_weights(in_weight, out_weight, up_weight, down_weight, vectors):
    columns = (
        lax.all_gather(in_weight, "fsdp", axis=1, tiled=True),
        lax.all_gather(out_weight, "fsdp", axis=1, tiled=True),
        lax.all_gather(up_weight, "fsdp", axis=1, tiled=True),
        lax.all_gather(down_weight, "fsdp", axis=1, tiled=True),
    )
    return (
        lax.all_gather(columns[0], ("dp", "seq"), axis=0, tiled=True),
        lax.all_gather(columns[1], ("dp", "seq"), axis=0, tiled=True),
        lax.all_gather(columns[2], ("dp", "seq"), axis=0, tiled=True),
        lax.all_gather(columns[3], ("dp", "seq"), axis=0, tiled=True),
        lax.all_gather(vectors[0], ("dp", "seq"), axis=0, tiled=True),
        lax.all_gather(vectors[1], ("dp", "seq"), axis=0, tiled=True),
        lax.all_gather(vectors[2], ("dp", "seq"), axis=0, tiled=True),
        lax.all_gather(vectors[3], ("dp", "seq"), axis=0, tiled=True),
        lax.all_gather(vectors[4], ("dp", "seq"), axis=0, tiled=True),
        lax.all_gather(vectors[5], ("dp", "seq"), axis=0, tiled=True),
        lax.all_gather(vectors[6], ("dp", "seq"), axis=0, tiled=True),
        lax.all_gather(vectors[7], ("dp", "seq"), axis=0, tiled=True),
    )


def reduce_rows(matrices, vectors):
    summed = (
        lax.psum_scatter(matrices[0], ("dp", "seq"), scatter_dimension=0, tiled=True),
        lax.psum_scatter(matrices[1], ("dp", "seq"), scatter_dimension=0, tiled=True),
        lax.psum_scatter(matrices[2], ("dp", "seq"), scatter_dimension=0, tiled=True),
        lax.psum_scatter(matrices[3], ("dp", "seq"), scatter_dimension=0, tiled=True),
        lax.psum_scatter(vectors[0], ("dp", "seq"), scatter_dimension=0, tiled=True),
        lax.psum_scatter(vectors[1], ("dp", "seq"), scatter_dimension=0, tiled=True),
        lax.psum_scatter(vectors[2], ("dp", "seq"), scatter_dimension=0, tiled=True),
        lax.psum_scatter(vectors[3], ("dp", "seq"), scatter_dimension=0, tiled=True),
        lax.psum_scatter(vectors[4], ("dp", "seq"), scatter_dimension=0, tiled=True),
        lax.psum_scatter(vectors[5], ("dp", "seq"), scatter_dimension=0, tiled=True),
        lax.psum_scatter(vectors[6], ("dp", "seq"), scatter_dimension=0, tiled=True),
        lax.psum_scatter(vectors[7], ("dp", "seq"), scatter_dimension=0, tiled=True),
    )
    return (summed[:4], summed[4:])


def reduce_cols(matrices, vectors):
    summed = (
        lax.psum_scatter(
            matrices[0].astype(jnp.bfloat16), "fsdp", scatter_dimension=1, tiled=True
        ).astype(jnp.float32),
        lax.psum_scatter(
            matrices[1].astype(jnp.bfloat16), "fsdp", scatter_dimension=1, tiled=True
        ).astype(jnp.float32),
        lax.psum_scatter(
            matrices[2].astype(jnp.bfloat16), "fsdp", scatter_dimension=1, tiled=True
        ).astype(jnp.float32),
        lax.psum_scatter(
            matrices[3].astype(jnp.bfloat16), "fsdp", scatter_dimension=1, tiled=True
        ).astype(jnp.float32),
    )
    totals = lax.psum(
        (
            vectors[0],
            vectors[1],
            vectors[2],
            vectors[3],
            vectors[4],
            vectors[5],
            vectors[6],
            vectors[7],
        ),
        "fsdp",
    )
    return (tuple(summed), tuple(totals))


def row_sum(values):
    return jnp.sum(values.astype(jnp.float32), axis=0)


def local(
    tokens,
    lengths,
    in_weight,
    in_bias,
    out_weight,
    out_bias,
    mid_gain,
    mid_shift,
    up_weight,
    up_bias,
    down_weight,
    down_bias,
    last_gain,
    last_shift,
    grad_output,
):
    seqs_local = tokens.shape[1]
    rows = tokens.shape[2]
    group_index = lax.axis_index("dp") * lax.axis_size("fsdp") + lax.axis_index("fsdp")
    factor = 1.0 / math.sqrt(HEAD)
    vectors = (in_bias, out_bias, mid_gain, mid_shift, up_bias, down_bias, last_gain, last_shift)
    acc_in = jnp.zeros((D, 3 * D), jnp.float32)
    acc_out = jnp.zeros((D, D), jnp.float32)
    acc_up = jnp.zeros((D, FF), jnp.float32)
    acc_down = jnp.zeros((FF, D), jnp.float32)
    vec_in = jnp.zeros((2 * D,), jnp.float32)
    vec_out = jnp.zeros((D,), jnp.float32)
    vec_mid_gain = jnp.zeros((D,), jnp.float32)
    vec_mid_shift = jnp.zeros((D,), jnp.float32)
    vec_up = jnp.zeros((FF,), jnp.float32)
    vec_down = jnp.zeros((D,), jnp.float32)
    vec_last_gain = jnp.zeros((D,), jnp.float32)
    vec_last_shift = jnp.zeros((D,), jnp.float32)
    results = []
    grad_inputs = []
    for micro in range(MICRO):
        weights = gather_weights(in_weight, out_weight, up_weight, down_weight, vectors)
        (
            in_matrix,
            out_matrix,
            up_matrix,
            down_matrix,
            in_vector,
            out_vector,
            mid_scale,
            mid_offset,
            up_vector,
            down_vector,
            last_scale,
            last_offset,
        ) = weights
        seq_lens = lax.dynamic_slice_in_dim(lengths[micro], group_index * seqs_local, seqs_local)
        flat = tokens[micro].reshape(-1, D)
        proj = jnp.dot(flat, in_matrix, preferred_element_type=jnp.float32) + with_key_zeros(
            in_vector
        )
        split = proj.astype(jnp.bfloat16).reshape(seqs_local, rows, HEADS, 3, HEAD)
        queries = split[:, :, :, 0]
        keys = split[:, :, :, 1].reshape(seqs_local, rows, D)
        values = split[:, :, :, 2].reshape(seqs_local, rows, D)
        peak_old = jnp.full((seqs_local, rows, HEADS), -1e30, jnp.float32)
        key_piece = lax.all_gather(keys, "seq", axis=1, tiled=True)
        value_piece = lax.all_gather(values, "seq", axis=1, tiled=True)
        count = key_piece.shape[1]
        key_piece = key_piece.reshape(seqs_local, count, HEADS, HEAD)
        value_piece = value_piece.reshape(seqs_local, count, HEADS, HEAD)
        scores = (
            jnp.einsum("sqhd,skhd->sqhk", queries, key_piece, preferred_element_type=jnp.float32)
            * factor
        )
        valid = jnp.arange(count, dtype=jnp.int32)[None, :] < seq_lens[:, None]
        scores = jnp.where(valid[:, None, None, :], scores, -jnp.inf)
        peak = jnp.maximum(peak_old, jnp.max(scores, axis=-1))
        weights_now = jnp.exp(scores - peak[..., None])
        total = jnp.sum(weights_now, axis=-1)
        summed = jnp.einsum(
            "sqhk,skhd->sqhd",
            weights_now.astype(jnp.bfloat16),
            value_piece,
            preferred_element_type=jnp.float32,
        )
        peak, total, summed = (peak, total, summed)
        attended = summed / total[..., None]
        log_total = peak + jnp.log(total)
        back_tokens = attended.astype(jnp.bfloat16).reshape(-1, D)
        mixed = jnp.dot(
            back_tokens, out_matrix, preferred_element_type=jnp.float32
        ) + out_vector.astype(jnp.float32)
        first_std, first_scale = standardize(flat.astype(jnp.float32) + mixed)
        normed = first_std * mid_scale.astype(jnp.float32) + mid_offset.astype(jnp.float32)
        normed_low = normed.astype(jnp.bfloat16)
        pre_up = jnp.dot(
            normed_low, up_matrix, preferred_element_type=jnp.float32
        ) + up_vector.astype(jnp.float32)
        act_low = jax.nn.gelu(pre_up, approximate=False).astype(jnp.bfloat16)
        branch = jnp.dot(
            act_low, down_matrix, preferred_element_type=jnp.float32
        ) + down_vector.astype(jnp.float32)
        second_std, second_scale = standardize(normed + branch)
        result = second_std * last_scale.astype(jnp.float32) + last_offset.astype(jnp.float32)
        results.append(result.astype(jnp.bfloat16).reshape(seqs_local, rows, D))
        back_weights = gather_weights(in_weight, out_weight, up_weight, down_weight, vectors)
        in_matrix, out_matrix, up_matrix, down_matrix = (
            back_weights[0],
            back_weights[1],
            back_weights[2],
            back_weights[3],
        )
        mid_scale, last_scale = (back_weights[6], back_weights[10])
        grad_top = grad_output[micro].reshape(-1, D).astype(jnp.float32)
        vec_last_gain = vec_last_gain + jnp.sum(grad_top * second_std, axis=0)
        vec_last_shift = vec_last_shift + jnp.sum(grad_top, axis=0)
        grad_second = norm_back(grad_top, second_std, second_scale, last_scale.astype(jnp.float32))
        grad_branch = grad_second.astype(jnp.bfloat16)
        vec_down = vec_down + row_sum(grad_branch)
        acc_down = acc_down + jnp.dot(act_low.T, grad_branch, preferred_element_type=jnp.float32)
        grad_pre = (
            jnp.dot(grad_branch, down_matrix.T, preferred_element_type=jnp.float32)
            * gelu_slope(pre_up)
        ).astype(jnp.bfloat16)
        vec_up = vec_up + row_sum(grad_pre)
        acc_up = acc_up + jnp.dot(normed_low.T, grad_pre, preferred_element_type=jnp.float32)
        grad_normed = grad_second + jnp.dot(
            grad_pre, up_matrix.T, preferred_element_type=jnp.float32
        )
        vec_mid_gain = vec_mid_gain + jnp.sum(grad_normed * first_std, axis=0)
        vec_mid_shift = vec_mid_shift + jnp.sum(grad_normed, axis=0)
        grad_first = norm_back(grad_normed, first_std, first_scale, mid_scale.astype(jnp.float32))
        grad_mixed = grad_first.astype(jnp.bfloat16)
        vec_out = vec_out + row_sum(grad_mixed)
        acc_out = acc_out + jnp.dot(back_tokens.T, grad_mixed, preferred_element_type=jnp.float32)
        grad_attended = jnp.dot(
            grad_mixed, out_matrix.T, preferred_element_type=jnp.float32
        ).astype(jnp.bfloat16)
        grad_heads = grad_attended.reshape(seqs_local, rows, HEADS, HEAD)
        delta = jnp.sum(grad_heads.astype(jnp.float32) * attended, axis=-1)
        attend_key_piece = lax.all_gather(keys, "seq", axis=1, tiled=True)
        attend_value_piece = lax.all_gather(values, "seq", axis=1, tiled=True)
        attend_count = attend_key_piece.shape[1]
        attend_key_piece = attend_key_piece.reshape(seqs_local, attend_count, HEADS, HEAD)
        attend_value_piece = attend_value_piece.reshape(seqs_local, attend_count, HEADS, HEAD)
        attend_valid = jnp.arange(attend_count, dtype=jnp.int32)[None, :] < seq_lens[:, None]
        score_scores = (
            jnp.einsum(
                "sqhd,skhd->sqhk", queries, attend_key_piece, preferred_element_type=jnp.float32
            )
            * factor
        )
        score_scores = jnp.where(attend_valid[:, None, None, :], score_scores, -jnp.inf)
        probs = jnp.exp(score_scores - log_total[..., None])
        grad_probs = jnp.einsum(
            "sqhd,skhd->sqhk", grad_heads, attend_value_piece, preferred_element_type=jnp.float32
        )
        grad_scores = (probs * (grad_probs - delta[..., None])).astype(jnp.bfloat16)
        grad_queries = (
            jnp.einsum(
                "sqhk,skhd->sqhd", grad_scores, attend_key_piece, preferred_element_type=jnp.float32
            )
            * factor
        )
        key_piece_grad = (
            jnp.einsum("sqhk,sqhd->skhd", grad_scores, queries, preferred_element_type=jnp.float32)
            * factor
        )
        value_piece_grad = jnp.einsum(
            "sqhk,sqhd->skhd",
            probs.astype(jnp.bfloat16),
            grad_heads,
            preferred_element_type=jnp.float32,
        )
        key_terms = key_piece_grad.reshape(seqs_local, attend_count, D)
        value_terms = value_piece_grad.reshape(seqs_local, attend_count, D)
        folded = (grad_queries, key_terms, value_terms)
        grad_queries, key_terms, value_terms = folded
        key_sums, value_sums = (
            lax.psum_scatter(
                key_terms.astype(jnp.bfloat16), "seq", scatter_dimension=1, tiled=True
            ).astype(jnp.float32),
            lax.psum_scatter(
                value_terms.astype(jnp.bfloat16), "seq", scatter_dimension=1, tiled=True
            ).astype(jnp.float32),
        )
        grad_stack = jnp.stack(
            [
                grad_queries,
                key_sums.reshape(seqs_local, rows, HEADS, HEAD),
                value_sums.reshape(seqs_local, rows, HEADS, HEAD),
            ],
            axis=3,
        )
        grad_proj = grad_stack.astype(jnp.bfloat16).reshape(-1, 3 * D)
        bias_terms = row_sum(grad_proj).reshape(HEADS, 3, HEAD)
        vec_in = vec_in + jnp.stack([bias_terms[:, 0], bias_terms[:, 2]], axis=1).reshape(2 * D)
        acc_in = acc_in + jnp.dot(flat.T, grad_proj, preferred_element_type=jnp.float32)
        grad_input = grad_first + jnp.dot(
            grad_proj, in_matrix.T, preferred_element_type=jnp.float32
        )
        grad_inputs.append(grad_input.reshape(seqs_local, rows, D))
    matrices = (acc_in, acc_out, acc_up, acc_down)
    vector_grads = (
        vec_in,
        vec_out,
        vec_mid_gain,
        vec_mid_shift,
        vec_up,
        vec_down,
        vec_last_gain,
        vec_last_shift,
    )
    matrices, vector_grads = reduce_rows(matrices, vector_grads)
    matrices, vector_grads = reduce_cols(matrices, vector_grads)
    return (
        jnp.stack(results, axis=0),
        jnp.stack(grad_inputs, axis=0),
        matrices[0],
        vector_grads[0],
        matrices[1],
        vector_grads[1],
        vector_grads[2],
        vector_grads[3],
        matrices[2],
        vector_grads[4],
        matrices[3],
        vector_grads[5],
        vector_grads[6],
        vector_grads[7],
    )


def project_kernel(x_ref, w_ref, b_ref, aux_ref, q_ref, k_ref, v_ref):
    rows = x_ref.shape[0]
    lane = lane_of((rows, 128))
    y = dot(x_ref[...], w_ref[0]) + b_ref[0]
    one = jnp.where(lane == 64, 1.0, 0.0)
    both = y[:, :128]
    q_ref[0] = jnp.where(lane < 64, both * (LOG2E / 8.0), one).astype(bf16)
    k_ref[0] = jnp.where(lane < 64, pltpu.roll(both, 64, 1), aux_ref[...].astype(f32)).astype(bf16)
    v_ref[0] = jnp.where(lane < 64, y[:, 128:], -1.0).astype(bf16)


def project(x, w, b, aux):
    span = x.shape[0]
    n = w.shape[0]
    head = pl.BlockSpec((1, span, 128), lambda h: (h, 0, 0))
    return pl.pallas_call(
        project_kernel,
        grid=(n,),
        in_specs=[
            pl.BlockSpec((span, D), lambda h: (0, 0)),
            pl.BlockSpec((1, D, 256), lambda h: (h, 0, 0)),
            pl.BlockSpec((1, 1, 256), lambda h: (h, 0, 0)),
            pl.BlockSpec((span, 128), lambda h: (0, 0)),
        ],
        out_specs=[head] * 3,
        out_shape=[jax.ShapeDtypeStruct((n, span, 128), bf16)] * 3,
        compiler_params=pltpu.CompilerParams(vmem_limit_bytes=56 * 2**20),
        cost_estimate=pl.CostEstimate(
            flops=n * span * D * 512, bytes_accessed=n * span * 768, transcendentals=0
        ),
        name="project",
    )(x, w, b, aux)


AXES = ("dp", "seq", "y", "c")
SWAP = [(0, 1), (1, 0)]


def piece_routes(pairs):
    first, second = [], []
    for z in range(4):
        for y in range(pairs):
            for c in range(2):
                source = (z * pairs + y) * 2 + c
                for micro in range(2):
                    target = ((2 * micro + c) * pairs + y) * 2 + z // 2
                    (first if micro == z % 2 else second).append((source, target))
    return first, second


def back(route):
    return [(target, source) for source, target in route]


def local_pairs(
    tokens,
    lengths,
    in_weight,
    in_bias,
    out_weight,
    out_bias,
    mid_gain,
    mid_shift,
    up_weight,
    up_bias,
    down_weight,
    down_bias,
    last_gain,
    last_shift,
    grad_output,
):
    rows = tokens.shape[2]
    pairs = lax.axis_size("y")
    blocks = lax.axis_size("dp") * lax.axis_size("seq")
    z = lax.axis_index("seq")
    y = lax.axis_index("y")
    c = lax.axis_index("c")
    odd = z % 2
    route_a, route_b = piece_routes(pairs)
    where_to = ("seq", "y", "c")

    def spread(array):
        own = lax.dynamic_index_in_dim(array[:, 0], odd, 0, keepdims=False)
        other = lax.dynamic_index_in_dim(array[:, 0], 1 - odd, 0, keepdims=False)
        return jnp.concatenate(
            [lax.ppermute(own, where_to, route_a), lax.ppermute(other, where_to, route_b)], axis=0
        )

    def collect(array):
        own = lax.ppermute(array[:rows], where_to, back(route_a))
        other = lax.ppermute(array[rows:], where_to, back(route_b))
        return jnp.stack(
            [jnp.where(odd == 0, own, other), jnp.where(odd == 0, other, own)], axis=0
        )[:, None]

    def swap(array):
        return lax.ppermute(array, "c", SWAP)

    vectors = (in_bias, out_bias, mid_gain, mid_shift, up_bias, down_bias, last_gain, last_shift)
    x = spread(tokens)
    packed = lax.all_gather(jnp.concatenate(vectors), ("dp", "seq"), axis=0, tiled=False)
    whole = []
    at = 0
    for v in vectors:
        whole.append(packed[:, at : at + v.shape[0]].reshape(-1).astype(f32))
        at += v.shape[0]
    in_vector, out_vector, mid_scale, mid_offset, up_vector, down_vector, last_scale, last_offset = whole

    w_in = lax.all_gather(in_weight, ("dp", "seq", "y"), axis=0, tiled=False)
    w_in = w_in.reshape(blocks, pairs, D // blocks, 3, 3, HEAD)
    n = pairs * 3

    def columns(weight):
        full = lax.all_gather(weight, AXES, axis=0, tiled=False)
        full = full.reshape(blocks, 2 * pairs, weight.shape[0], weight.shape[1])
        return full.transpose(0, 2, 1, 3).reshape(blocks * weight.shape[0], -1)

    w_out = columns(out_weight)
    w_up = columns(up_weight)
    w_down = columns(down_weight)
    g_top = spread(grad_output)

    micro = z // 2
    group = (lax.axis_index("dp") * pairs + y) * 2 + odd
    length = lengths[micro, group]
    iota = jnp.arange(rows, dtype=jnp.int32)

    def places(core):
        return [(2 * core + micro) * rows + iota, (2 * core + 1 - micro) * rows + iota]

    place = jnp.concatenate(places(c) + places(1 - c))
    mask = jnp.where(place < length, 0.0, -1e30).astype(bf16)
    span = 4 * rows
    half = 2 * rows
    lane = jnp.arange(128, dtype=jnp.int32)[None, :]
    aux = jnp.where(
        lane == 64, mask[:, None], jnp.where((lane > 64) & (lane < 68), -1.0, 0.0).astype(bf16)
    )

    x_full = jnp.concatenate([x, swap(x)], axis=0)
    w_head = jnp.pad(
        w_in.transpose(1, 3, 0, 2, 4, 5).reshape(n, D, 192), ((0, 0), (0, 0), (0, 64))
    )
    bias = lax.dynamic_index_in_dim(
        in_vector.reshape(pairs, 2, 3, 2, HEAD), c, 1, keepdims=False
    ).reshape(n, 2, HEAD)
    b_head = jnp.concatenate(
        [bias[:, 0], jnp.zeros_like(bias[:, 0]), bias[:, 1], jnp.zeros_like(bias[:, 0])], axis=1
    )[:, None]
    q, k, v = project(x_full, w_head, b_head, aux)
    attended, q = attend(q, k, v)
    mine = attended[:half]
    theirs = swap(attended[half:])

    def by_core(own, other):
        even = jnp.where(c == 0, own, other).reshape(half, pairs, 1, 192)
        odd_ = jnp.where(c == 0, other, own).reshape(half, pairs, 1, 192)
        return jnp.concatenate([even, odd_], axis=2).reshape(half, D)

    att = by_core(mine, theirs)
    mixed = dot(att, w_out) + out_vector
    first_std, first_scale = standardize(x.astype(f32) + mixed)
    normed = first_std * mid_scale + mid_offset
    normed_low = normed.astype(bf16)
    pre_up = dot(normed_low, w_up) + up_vector
    act_low = jax.nn.gelu(pre_up, approximate=False).astype(bf16)
    branch = dot(act_low, w_down) + down_vector
    second_std, second_scale = standardize(normed + branch)
    result = collect((second_std * last_scale + last_offset).astype(bf16))

    g_top = g_top.astype(f32)
    vec_last_gain = jnp.sum(g_top * second_std, axis=0)
    vec_last_shift = jnp.sum(g_top, axis=0)
    grad_second = norm_back(g_top, second_std, second_scale, last_scale)
    grad_branch = grad_second.astype(bf16)
    vec_down = row_sum(grad_branch)
    grad_down = dot(act_low, grad_branch, TN)
    grad_pre = (dot(grad_branch, w_down, NT) * gelu_slope(pre_up)).astype(bf16)
    vec_up = row_sum(grad_pre)
    grad_up = dot(normed_low, grad_pre, TN)
    grad_normed = grad_second + dot(grad_pre, w_up, NT)
    vec_mid_gain = jnp.sum(grad_normed * first_std, axis=0)
    vec_mid_shift = jnp.sum(grad_normed, axis=0)
    grad_first = norm_back(grad_normed, first_std, first_scale, mid_scale)
    grad_mixed = grad_first.astype(bf16)
    vec_out = row_sum(grad_mixed)
    grad_out = dot(att, grad_mixed, TN)
    grad_att = dot(grad_mixed, w_out, NT).astype(bf16).reshape(half, pairs, 2, 192)
    g_even = grad_att[:, :, 0].reshape(half, n * HEAD)
    g_odd = grad_att[:, :, 1].reshape(half, n * HEAD)
    g_own = jnp.where(c == 0, g_even, g_odd)
    g_other = swap(jnp.where(c == 0, g_odd, g_even))
    dq, dk, dv = attend_back(q, k, v, attended, jnp.concatenate([g_own, g_other], axis=0))

    def scatter(grad, weight):
        r, w = weight.shape
        grad = grad.astype(bf16).reshape(blocks, r, 2 * pairs, w).transpose(0, 2, 1, 3)
        return lax.psum_scatter(
            grad.reshape(2 * pairs * blocks, r, w), AXES, scatter_dimension=0, tiled=True
        )[0].astype(f32)

    out_down = scatter(grad_down, down_weight)
    out_up = scatter(grad_up, up_weight)
    out_out = scatter(grad_out, out_weight)
    grad_proj = jnp.concatenate([dq, dk, dv], axis=1)
    grad_in = dot(x_full, grad_proj, TN).astype(bf16)
    r = in_weight.shape[0]
    grad_in = grad_in.reshape(blocks, r, 3, pairs, 192).transpose(0, 3, 1, 2, 4)
    out_in = lax.psum_scatter(
        grad_in.reshape(blocks * pairs, r, 576), ("dp", "seq", "y"), scatter_dimension=0, tiled=True
    )[0]
    out_in = out_in.reshape(r, 3, 3, HEAD).transpose(0, 2, 1, 3).reshape(r, 576).astype(f32)
    w_kind = w_in.transpose(0, 2, 4, 1, 3, 5).reshape(D, 3 * n * HEAD)
    grad_x = dot(grad_proj, w_kind, NT)
    grad_x = grad_first + grad_x[:half] + swap(grad_x[half:].astype(bf16)).astype(f32)
    grad_tokens = collect(grad_x.astype(bf16)).astype(f32)
    own_bias = jnp.stack(
        [row_sum(dq).reshape(pairs, 3, HEAD), row_sum(dv).reshape(pairs, 3, HEAD)], axis=2
    )
    core = (jnp.arange(2) == c).astype(f32)
    vec_in = (own_bias[:, None] * core[None, :, None, None, None]).reshape(-1)
    grads = (
        vec_in,
        vec_out,
        vec_mid_gain,
        vec_mid_shift,
        vec_up,
        vec_down,
        vec_last_gain,
        vec_last_shift,
    )
    packed = jnp.concatenate([g.reshape(blocks, -1) for g in grads], axis=1)
    total = lax.psum(packed, AXES)
    total = lax.dynamic_index_in_dim(
        total, lax.axis_index("dp") * lax.axis_size("seq") + z, 0, keepdims=False
    )
    sums = []
    at = 0
    for vector in vectors:
        sums.append(total[at : at + vector.shape[0]])
        at += vector.shape[0]
    return (
        result,
        grad_tokens,
        out_in,
        sums[0],
        out_out,
        sums[1],
        sums[2],
        sums[3],
        out_up,
        sums[4],
        out_down,
        sums[5],
        sums[6],
        sums[7],
    )


def specs(fsdp):
    data = P(None, ("dp",) + fsdp, "seq", None)
    matrix = P(("dp", "seq"), fsdp)
    vector = P(("dp", "seq"))
    ins = (data, P(), matrix, vector, matrix, vector, vector, vector, matrix, vector, matrix, vector)
    ins += (vector, vector, data)
    outs = (data, data, matrix, vector, matrix, vector, vector, vector, matrix, vector, matrix)
    outs += (vector, vector, vector)
    return ins, outs


def solution(mesh):
    dp, seq, fsdp = (mesh.shape[name] for name in ("dp", "seq", "fsdp"))
    if seq == 2 * MICRO and fsdp % 2 == 0:
        mesh = jax.sharding.Mesh(mesh.devices.reshape(dp, seq, fsdp // 2, 2), AXES)
        body, (ins, outs) = local_pairs, specs(("y", "c"))
    else:
        body, (ins, outs) = local, specs(("fsdp",))
    return jax.shard_map(body, mesh=mesh, in_specs=ins, out_specs=outs, check_vma=False)
```

```python
import math
import jax
import jax.numpy as jnp
from jax import lax
from jax.experimental import pallas as pl
from jax.experimental.pallas import tpu as pltpu
from jax.sharding import PartitionSpec as P

D = 768
HEADS = 12
HEAD = 64
FF = 3072
MICRO = 2
LOG2E = math.log2(math.e)
NT = (((1,), (1,)), ((), ()))
TN = (((0,), (0,)), ((), ()))
f32 = jnp.float32
bf16 = jnp.bfloat16


def dot(a, b, dims=(((1,), (0,)), ((), ()))):
    return lax.dot_general(a, b, dims, preferred_element_type=f32)


def lane_of(shape):
    return lax.broadcasted_iota(jnp.int32, shape, 1)


def attend_kernel(q_ref, k_ref, v_ref, o_ref, qa_ref):
    rows = q_ref.shape[1]
    lane = lane_of((rows, 128))
    halves = []
    for h in range(2):
        q = q_ref[h]
        s = dot(q, k_ref[h], NT)
        top = jnp.max(s, axis=-1, keepdims=True)
        p = jnp.exp2(s - top).astype(bf16)
        o = dot(p, v_ref[h])
        total = -o[:, 64:65]
        halves.append(o / total)
        level = top + jnp.log2(total)
        high = level.astype(bf16)
        rest = level - high.astype(f32)
        mid = rest.astype(bf16)
        low = (rest - mid.astype(f32)).astype(bf16)
        qa_ref[h] = jnp.where(
            lane < 65,
            q.astype(f32),
            jnp.where(
                lane == 65,
                high.astype(f32),
                jnp.where(lane == 66, mid.astype(f32), jnp.where(lane == 67, low.astype(f32), 0.0)),
            ),
        ).astype(bf16)
    o_ref[...] = jnp.where(lane < 64, halves[0], pltpu.roll(halves[1], 64, 1)).astype(bf16)


def attend(q, k, v, block=512):
    n, span, _ = q.shape
    whole = pl.BlockSpec((2, span, 128), lambda p, i: (p, 0, 0))
    part = pl.BlockSpec((2, block, 128), lambda p, i: (p, i, 0))
    return pl.pallas_call(
        attend_kernel,
        grid=(n // 2, span // block),
        in_specs=[part, whole, whole],
        out_specs=[pl.BlockSpec((block, 128), lambda p, i: (i, p)), part],
        out_shape=[
            jax.ShapeDtypeStruct((span, n * 64), bf16),
            jax.ShapeDtypeStruct((n, span, 128), bf16),
        ],
        compiler_params=pltpu.CompilerParams(vmem_limit_bytes=56 * 2**20),
        cost_estimate=pl.CostEstimate(
            flops=n * span * span * 512, bytes_accessed=n * span * 1024, transcendentals=n * span * span
        ),
        name="attend",
    )(q, k, v)


def attend_back_kernel(q_ref, k_ref, v_ref, o_ref, g_ref, dq_ref, dk_ref, dv_ref, ga_ref, acc_ref):
    step = pl.program_id(1)
    span = q_ref.shape[1]
    rows = k_ref.shape[1]

    @pl.when(step == 0)
    def _():
        lane = lane_of((span, 128))
        grad = g_ref[...].astype(f32)
        prod = grad * o_ref[...].astype(f32)
        for h in range(2):
            mine = (lane < 64) if h == 0 else (lane >= 64)
            delta = jnp.sum(jnp.where(mine, prod, 0.0), axis=-1, keepdims=True)
            high = delta.astype(bf16).astype(f32)
            mid = delta - high
            g = grad if h == 0 else pltpu.roll(grad, 64, 1)
            ga_ref[h] = jnp.where(
                lane < 64, g, jnp.where(lane == 64, high, jnp.where(lane == 65, mid, 0.0))
            ).astype(bf16)
        acc_ref[...] = jnp.zeros_like(acc_ref)

    lane = lane_of((rows, 128))
    dks, dvs = [], []
    for h in range(2):
        q = q_ref[h]
        k = k_ref[h]
        g = ga_ref[h]
        p = jnp.exp2(dot(k, q, NT))
        ds = (p * dot(v_ref[h], g, NT)).astype(bf16)
        dvs.append(dot(p.astype(bf16), g))
        dks.append(dot(ds, q))
        acc_ref[h] += dot(ds, k, TN)
    dk_ref[...] = (jnp.where(lane < 64, dks[0], pltpu.roll(dks[1], 64, 1)) * (1.0 / LOG2E)).astype(bf16)
    dv_ref[...] = jnp.where(lane < 64, dvs[0], pltpu.roll(dvs[1], 64, 1)).astype(bf16)

    @pl.when(step == pl.num_programs(1) - 1)
    def _():
        wide = lane_of((span, 128))
        dq_ref[...] = (jnp.where(wide < 64, acc_ref[0], pltpu.roll(acc_ref[1], 64, 1)) * 0.125).astype(bf16)


def attend_back(q, k, v, o, g, block=256):
    n, span, _ = q.shape
    whole = pl.BlockSpec((2, span, 128), lambda p, i: (p, 0, 0))
    part = pl.BlockSpec((2, block, 128), lambda p, i: (p, i, 0))
    flat = pl.BlockSpec((span, 128), lambda p, i: (0, p))
    rows = pl.BlockSpec((block, 128), lambda p, i: (i, p))
    return pl.pallas_call(
        attend_back_kernel,
        grid=(n // 2, span // block),
        in_specs=[whole, part, part, flat, flat],
        out_specs=[flat, rows, rows],
        out_shape=[jax.ShapeDtypeStruct((span, n * 64), bf16)] * 3,
        scratch_shapes=[pltpu.VMEM((2, span, 128), bf16), pltpu.VMEM((2, span, 128), f32)],
        compiler_params=pltpu.CompilerParams(vmem_limit_bytes=56 * 2**20),
        cost_estimate=pl.CostEstimate(
            flops=n * span * span * 1280, bytes_accessed=n * span * 1024, transcendentals=n * span * span
        ),
        name="attend_back",
    )(q, k, v, o, g)


epsilon = 1e-05


def standardize(hidden):
    centered = hidden - jnp.mean(hidden, axis=-1, keepdims=True)
    scale = lax.rsqrt(jnp.mean(centered * centered, axis=-1, keepdims=True) + epsilon)
    return (centered * scale, scale)


def norm_back(grad_out, standard, scale, gain):
    spread = grad_out * gain
    return scale * (
        spread
        - jnp.mean(spread, axis=-1, keepdims=True)
        - standard * jnp.mean(spread * standard, axis=-1, keepdims=True)
    )


def gelu_slope(value):
    return 0.5 * (1.0 + lax.erf(value * (1.0 / math.sqrt(2.0)))) + value * jnp.exp(
        -0.5 * value * value
    ) * (1.0 / math.sqrt(2.0 * math.pi))


def with_key_zeros(query_value):
    paired = query_value.astype(jnp.float32).reshape(HEADS, 2, HEAD)
    return jnp.stack([paired[:, 0], jnp.zeros_like(paired[:, 0]), paired[:, 1]], axis=1).reshape(
        3 * D
    )


def gather_weights(in_weight, out_weight, up_weight, down_weight, vectors):
    columns = (
        lax.all_gather(in_weight, "fsdp", axis=1, tiled=True),
        lax.all_gather(out_weight, "fsdp", axis=1, tiled=True),
        lax.all_gather(up_weight, "fsdp", axis=1, tiled=True),
        lax.all_gather(down_weight, "fsdp", axis=1, tiled=True),
    )
    return (
        lax.all_gather(columns[0], ("dp", "seq"), axis=0, tiled=True),
        lax.all_gather(columns[1], ("dp", "seq"), axis=0, tiled=True),
        lax.all_gather(columns[2], ("dp", "seq"), axis=0, tiled=True),
        lax.all_gather(columns[3], ("dp", "seq"), axis=0, tiled=True),
        lax.all_gather(vectors[0], ("dp", "seq"), axis=0, tiled=True),
        lax.all_gather(vectors[1], ("dp", "seq"), axis=0, tiled=True),
        lax.all_gather(vectors[2], ("dp", "seq"), axis=0, tiled=True),
        lax.all_gather(vectors[3], ("dp", "seq"), axis=0, tiled=True),
        lax.all_gather(vectors[4], ("dp", "seq"), axis=0, tiled=True),
        lax.all_gather(vectors[5], ("dp", "seq"), axis=0, tiled=True),
        lax.all_gather(vectors[6], ("dp", "seq"), axis=0, tiled=True),
        lax.all_gather(vectors[7], ("dp", "seq"), axis=0, tiled=True),
    )


def reduce_rows(matrices, vectors):
    summed = (
        lax.psum_scatter(matrices[0], ("dp", "seq"), scatter_dimension=0, tiled=True),
        lax.psum_scatter(matrices[1], ("dp", "seq"), scatter_dimension=0, tiled=True),
        lax.psum_scatter(matrices[2], ("dp", "seq"), scatter_dimension=0, tiled=True),
        lax.psum_scatter(matrices[3], ("dp", "seq"), scatter_dimension=0, tiled=True),
        lax.psum_scatter(vectors[0], ("dp", "seq"), scatter_dimension=0, tiled=True),
        lax.psum_scatter(vectors[1], ("dp", "seq"), scatter_dimension=0, tiled=True),
        lax.psum_scatter(vectors[2], ("dp", "seq"), scatter_dimension=0, tiled=True),
        lax.psum_scatter(vectors[3], ("dp", "seq"), scatter_dimension=0, tiled=True),
        lax.psum_scatter(vectors[4], ("dp", "seq"), scatter_dimension=0, tiled=True),
        lax.psum_scatter(vectors[5], ("dp", "seq"), scatter_dimension=0, tiled=True),
        lax.psum_scatter(vectors[6], ("dp", "seq"), scatter_dimension=0, tiled=True),
        lax.psum_scatter(vectors[7], ("dp", "seq"), scatter_dimension=0, tiled=True),
    )
    return (summed[:4], summed[4:])


def reduce_cols(matrices, vectors):
    summed = (
        lax.psum_scatter(
            matrices[0].astype(jnp.bfloat16), "fsdp", scatter_dimension=1, tiled=True
        ).astype(jnp.float32),
        lax.psum_scatter(
            matrices[1].astype(jnp.bfloat16), "fsdp", scatter_dimension=1, tiled=True
        ).astype(jnp.float32),
        lax.psum_scatter(
            matrices[2].astype(jnp.bfloat16), "fsdp", scatter_dimension=1, tiled=True
        ).astype(jnp.float32),
        lax.psum_scatter(
            matrices[3].astype(jnp.bfloat16), "fsdp", scatter_dimension=1, tiled=True
        ).astype(jnp.float32),
    )
    totals = lax.psum(
        (
            vectors[0],
            vectors[1],
            vectors[2],
            vectors[3],
            vectors[4],
            vectors[5],
            vectors[6],
            vectors[7],
        ),
        "fsdp",
    )
    return (tuple(summed), tuple(totals))


def row_sum(values):
    return jnp.sum(values.astype(jnp.float32), axis=0)


def local(
    tokens,
    lengths,
    in_weight,
    in_bias,
    out_weight,
    out_bias,
    mid_gain,
    mid_shift,
    up_weight,
    up_bias,
    down_weight,
    down_bias,
    last_gain,
    last_shift,
    grad_output,
):
    seqs_local = tokens.shape[1]
    rows = tokens.shape[2]
    group_index = lax.axis_index("dp") * lax.axis_size("fsdp") + lax.axis_index("fsdp")
    factor = 1.0 / math.sqrt(HEAD)
    vectors = (in_bias, out_bias, mid_gain, mid_shift, up_bias, down_bias, last_gain, last_shift)
    acc_in = jnp.zeros((D, 3 * D), jnp.float32)
    acc_out = jnp.zeros((D, D), jnp.float32)
    acc_up = jnp.zeros((D, FF), jnp.float32)
    acc_down = jnp.zeros((FF, D), jnp.float32)
    vec_in = jnp.zeros((2 * D,), jnp.float32)
    vec_out = jnp.zeros((D,), jnp.float32)
    vec_mid_gain = jnp.zeros((D,), jnp.float32)
    vec_mid_shift = jnp.zeros((D,), jnp.float32)
    vec_up = jnp.zeros((FF,), jnp.float32)
    vec_down = jnp.zeros((D,), jnp.float32)
    vec_last_gain = jnp.zeros((D,), jnp.float32)
    vec_last_shift = jnp.zeros((D,), jnp.float32)
    results = []
    grad_inputs = []
    for micro in range(MICRO):
        weights = gather_weights(in_weight, out_weight, up_weight, down_weight, vectors)
        (
            in_matrix,
            out_matrix,
            up_matrix,
            down_matrix,
            in_vector,
            out_vector,
            mid_scale,
            mid_offset,
            up_vector,
            down_vector,
            last_scale,
            last_offset,
        ) = weights
        seq_lens = lax.dynamic_slice_in_dim(lengths[micro], group_index * seqs_local, seqs_local)
        flat = tokens[micro].reshape(-1, D)
        proj = jnp.dot(flat, in_matrix, preferred_element_type=jnp.float32) + with_key_zeros(
            in_vector
        )
        split = proj.astype(jnp.bfloat16).reshape(seqs_local, rows, HEADS, 3, HEAD)
        queries = split[:, :, :, 0]
        keys = split[:, :, :, 1].reshape(seqs_local, rows, D)
        values = split[:, :, :, 2].reshape(seqs_local, rows, D)
        peak_old = jnp.full((seqs_local, rows, HEADS), -1e30, jnp.float32)
        key_piece = lax.all_gather(keys, "seq", axis=1, tiled=True)
        value_piece = lax.all_gather(values, "seq", axis=1, tiled=True)
        count = key_piece.shape[1]
        key_piece = key_piece.reshape(seqs_local, count, HEADS, HEAD)
        value_piece = value_piece.reshape(seqs_local, count, HEADS, HEAD)
        scores = (
            jnp.einsum("sqhd,skhd->sqhk", queries, key_piece, preferred_element_type=jnp.float32)
            * factor
        )
        valid = jnp.arange(count, dtype=jnp.int32)[None, :] < seq_lens[:, None]
        scores = jnp.where(valid[:, None, None, :], scores, -jnp.inf)
        peak = jnp.maximum(peak_old, jnp.max(scores, axis=-1))
        weights_now = jnp.exp(scores - peak[..., None])
        total = jnp.sum(weights_now, axis=-1)
        summed = jnp.einsum(
            "sqhk,skhd->sqhd",
            weights_now.astype(jnp.bfloat16),
            value_piece,
            preferred_element_type=jnp.float32,
        )
        peak, total, summed = (peak, total, summed)
        attended = summed / total[..., None]
        log_total = peak + jnp.log(total)
        back_tokens = attended.astype(jnp.bfloat16).reshape(-1, D)
        mixed = jnp.dot(
            back_tokens, out_matrix, preferred_element_type=jnp.float32
        ) + out_vector.astype(jnp.float32)
        first_std, first_scale = standardize(flat.astype(jnp.float32) + mixed)
        normed = first_std * mid_scale.astype(jnp.float32) + mid_offset.astype(jnp.float32)
        normed_low = normed.astype(jnp.bfloat16)
        pre_up = jnp.dot(
            normed_low, up_matrix, preferred_element_type=jnp.float32
        ) + up_vector.astype(jnp.float32)
        act_low = jax.nn.gelu(pre_up, approximate=False).astype(jnp.bfloat16)
        branch = jnp.dot(
            act_low, down_matrix, preferred_element_type=jnp.float32
        ) + down_vector.astype(jnp.float32)
        second_std, second_scale = standardize(normed + branch)
        result = second_std * last_scale.astype(jnp.float32) + last_offset.astype(jnp.float32)
        results.append(result.astype(jnp.bfloat16).reshape(seqs_local, rows, D))
        back_weights = gather_weights(in_weight, out_weight, up_weight, down_weight, vectors)
        in_matrix, out_matrix, up_matrix, down_matrix = (
            back_weights[0],
            back_weights[1],
            back_weights[2],
            back_weights[3],
        )
        mid_scale, last_scale = (back_weights[6], back_weights[10])
        grad_top = grad_output[micro].reshape(-1, D).astype(jnp.float32)
        vec_last_gain = vec_last_gain + jnp.sum(grad_top * second_std, axis=0)
        vec_last_shift = vec_last_shift + jnp.sum(grad_top, axis=0)
        grad_second = norm_back(grad_top, second_std, second_scale, last_scale.astype(jnp.float32))
        grad_branch = grad_second.astype(jnp.bfloat16)
        vec_down = vec_down + row_sum(grad_branch)
        acc_down = acc_down + jnp.dot(act_low.T, grad_branch, preferred_element_type=jnp.float32)
        grad_pre = (
            jnp.dot(grad_branch, down_matrix.T, preferred_element_type=jnp.float32)
            * gelu_slope(pre_up)
        ).astype(jnp.bfloat16)
        vec_up = vec_up + row_sum(grad_pre)
        acc_up = acc_up + jnp.dot(normed_low.T, grad_pre, preferred_element_type=jnp.float32)
        grad_normed = grad_second + jnp.dot(
            grad_pre, up_matrix.T, preferred_element_type=jnp.float32
        )
        vec_mid_gain = vec_mid_gain + jnp.sum(grad_normed * first_std, axis=0)
        vec_mid_shift = vec_mid_shift + jnp.sum(grad_normed, axis=0)
        grad_first = norm_back(grad_normed, first_std, first_scale, mid_scale.astype(jnp.float32))
        grad_mixed = grad_first.astype(jnp.bfloat16)
        vec_out = vec_out + row_sum(grad_mixed)
        acc_out = acc_out + jnp.dot(back_tokens.T, grad_mixed, preferred_element_type=jnp.float32)
        grad_attended = jnp.dot(
            grad_mixed, out_matrix.T, preferred_element_type=jnp.float32
        ).astype(jnp.bfloat16)
        grad_heads = grad_attended.reshape(seqs_local, rows, HEADS, HEAD)
        delta = jnp.sum(grad_heads.astype(jnp.float32) * attended, axis=-1)
        attend_key_piece = lax.all_gather(keys, "seq", axis=1, tiled=True)
        attend_value_piece = lax.all_gather(values, "seq", axis=1, tiled=True)
        attend_count = attend_key_piece.shape[1]
        attend_key_piece = attend_key_piece.reshape(seqs_local, attend_count, HEADS, HEAD)
        attend_value_piece = attend_value_piece.reshape(seqs_local, attend_count, HEADS, HEAD)
        attend_valid = jnp.arange(attend_count, dtype=jnp.int32)[None, :] < seq_lens[:, None]
        score_scores = (
            jnp.einsum(
                "sqhd,skhd->sqhk", queries, attend_key_piece, preferred_element_type=jnp.float32
            )
            * factor
        )
        score_scores = jnp.where(attend_valid[:, None, None, :], score_scores, -jnp.inf)
        probs = jnp.exp(score_scores - log_total[..., None])
        grad_probs = jnp.einsum(
            "sqhd,skhd->sqhk", grad_heads, attend_value_piece, preferred_element_type=jnp.float32
        )
        grad_scores = (probs * (grad_probs - delta[..., None])).astype(jnp.bfloat16)
        grad_queries = (
            jnp.einsum(
                "sqhk,skhd->sqhd", grad_scores, attend_key_piece, preferred_element_type=jnp.float32
            )
            * factor
        )
        key_piece_grad = (
            jnp.einsum("sqhk,sqhd->skhd", grad_scores, queries, preferred_element_type=jnp.float32)
            * factor
        )
        value_piece_grad = jnp.einsum(
            "sqhk,sqhd->skhd",
            probs.astype(jnp.bfloat16),
            grad_heads,
            preferred_element_type=jnp.float32,
        )
        key_terms = key_piece_grad.reshape(seqs_local, attend_count, D)
        value_terms = value_piece_grad.reshape(seqs_local, attend_count, D)
        folded = (grad_queries, key_terms, value_terms)
        grad_queries, key_terms, value_terms = folded
        key_sums, value_sums = (
            lax.psum_scatter(
                key_terms.astype(jnp.bfloat16), "seq", scatter_dimension=1, tiled=True
            ).astype(jnp.float32),
            lax.psum_scatter(
                value_terms.astype(jnp.bfloat16), "seq", scatter_dimension=1, tiled=True
            ).astype(jnp.float32),
        )
        grad_stack = jnp.stack(
            [
                grad_queries,
                key_sums.reshape(seqs_local, rows, HEADS, HEAD),
                value_sums.reshape(seqs_local, rows, HEADS, HEAD),
            ],
            axis=3,
        )
        grad_proj = grad_stack.astype(jnp.bfloat16).reshape(-1, 3 * D)
        bias_terms = row_sum(grad_proj).reshape(HEADS, 3, HEAD)
        vec_in = vec_in + jnp.stack([bias_terms[:, 0], bias_terms[:, 2]], axis=1).reshape(2 * D)
        acc_in = acc_in + jnp.dot(flat.T, grad_proj, preferred_element_type=jnp.float32)
        grad_input = grad_first + jnp.dot(
            grad_proj, in_matrix.T, preferred_element_type=jnp.float32
        )
        grad_inputs.append(grad_input.reshape(seqs_local, rows, D))
    matrices = (acc_in, acc_out, acc_up, acc_down)
    vector_grads = (
        vec_in,
        vec_out,
        vec_mid_gain,
        vec_mid_shift,
        vec_up,
        vec_down,
        vec_last_gain,
        vec_last_shift,
    )
    matrices, vector_grads = reduce_rows(matrices, vector_grads)
    matrices, vector_grads = reduce_cols(matrices, vector_grads)
    return (
        jnp.stack(results, axis=0),
        jnp.stack(grad_inputs, axis=0),
        matrices[0],
        vector_grads[0],
        matrices[1],
        vector_grads[1],
        vector_grads[2],
        vector_grads[3],
        matrices[2],
        vector_grads[4],
        matrices[3],
        vector_grads[5],
        vector_grads[6],
        vector_grads[7],
    )


def half_tiles(first, second):
    lane = lane_of(first.shape)
    return jnp.where(lane < 64, first, second)


def turn(tile):
    return pltpu.roll(tile, 64, 1)


def join_columns(parts):
    tiles = []
    for a, b in (parts[:2], parts[2:]):
        low = turn(b[:, :128])
        tiles += [a[:, :128], half_tiles(a[:, 128:], low), half_tiles(low, turn(b[:, 128:]))]
    return jnp.concatenate(tiles, axis=1)


def part_columns(full):
    parts = []
    for pair in range(full.shape[1] // 384):
        t = [full[:, pair * 384 + i * 128 : pair * 384 + i * 128 + 128] for i in range(3)]
        zero = jnp.zeros_like(t[0])
        parts.append(jnp.concatenate([t[0], half_tiles(t[1], zero)], axis=1))
        mid = turn(t[2])
        parts.append(jnp.concatenate([half_tiles(turn(t[1]), mid), half_tiles(mid, zero)], axis=1))
    return parts


def params(**kw):
    return pltpu.CompilerParams(vmem_limit_bytes=58 * 2**20, **kw)


ANY = pl.BlockSpec(memory_space=pl.ANY)


def project_kernel(me_ref, x_ref, b_ref, aux_ref, *rest):
    pieces, (q_ref, k_ref, v_ref, w_ref, held, sems) = rest[:4], rest[4:]
    head = pl.program_id(0)
    xz = me_ref[0]

    def copies():
        for dx in range(2):
            for dy in range(2):
                for dz in range(4):
                    yield pltpu.make_async_copy(
                        pieces[dx * 2 + dy].at[dz],
                        held.at[lax.bitwise_xor(xz, dx * 4 + dz), pl.ds(dy * 3, 3)],
                        sems.at[dx * 8 + dy * 4 + dz],
                    )

    @pl.when(head == 0)
    def _():
        for copy in copies():
            copy.start()
        for copy in copies():
            copy.wait()

    rows = x_ref.shape[0]
    lane = lane_of((rows, 128))
    y = dot(x_ref[...], held[:, head].reshape(D, 256)) + b_ref[0]
    one = jnp.where(lane == 64, 1.0, 0.0)
    both = y[:, :128]
    q_ref[0] = jnp.where(lane < 64, both * (LOG2E / 8.0), one).astype(bf16)
    k_ref[0] = jnp.where(lane < 64, turn(both), aux_ref[...].astype(f32)).astype(bf16)
    v_ref[0] = jnp.where(lane < 64, y[:, 128:], -1.0).astype(bf16)

    @pl.when(head == pl.num_programs(0) - 1)
    def _():
        for p in range(3):
            a = held[:, 2 * p].reshape(D, 256).astype(f32)
            b = held[:, 2 * p + 1].reshape(D, 256).astype(f32)
            a0, a1, b0, b1 = a[:, :128], a[:, 128:], b[:, :128], b[:, 128:]
            w_ref[:, p * 128 : p * 128 + 128] = half_tiles(a0, turn(b0)).astype(bf16)
            w_ref[:, 384 + p * 128 : 512 + p * 128] = half_tiles(turn(a0), b0).astype(bf16)
            w_ref[:, 768 + p * 128 : 896 + p * 128] = half_tiles(a1, turn(b1)).astype(bf16)


def project(me, x, b, aux, pieces):
    span = x.shape[0]
    n = b.shape[0]
    head = pl.BlockSpec((1, span, 128), lambda h, m: (h, 0, 0))
    return pl.pallas_call(
        project_kernel,
        grid_spec=pltpu.PrefetchScalarGridSpec(
            num_scalar_prefetch=1,
            grid=(n,),
            in_specs=[
                pl.BlockSpec((span, D), lambda h, m: (0, 0)),
                pl.BlockSpec((1, 1, 256), lambda h, m: (h, 0, 0)),
                pl.BlockSpec((span, 128), lambda h, m: (0, 0)),
            ]
            + [ANY] * 4,
            out_specs=[head] * 3 + [pl.BlockSpec((D, 1152), lambda h, m: (0, 0))],
            scratch_shapes=[pltpu.VMEM((8, n, 96, 256), bf16), pltpu.SemaphoreType.DMA((16,))],
        ),
        out_shape=[jax.ShapeDtypeStruct((n, span, 128), bf16)] * 3
        + [jax.ShapeDtypeStruct((D, 1152), bf16)],
        compiler_params=params(),
        cost_estimate=pl.CostEstimate(
            flops=n * span * D * 512, bytes_accessed=n * span * 768, transcendentals=0
        ),
        name="project",
    )(me, x, b, aux, *pieces)


def center(hidden):
    centered = hidden - jnp.mean(hidden, axis=-1, keepdims=True)
    scale = lax.rsqrt(jnp.mean(centered * centered, axis=-1, keepdims=True) + epsilon)
    return centered * scale, scale


def middle_kernel(me_ref, x_ref, mine_ref, theirs_ref, g_ref, vec_ref, upb_ref, *rest):
    up_p, down_p, out_p = rest[:8], rest[8:16], rest[16:24]
    (
        y_ref,
        nl_ref,
        act_ref,
        gb_ref,
        gp_ref,
        gm_ref,
        gf_ref,
        ga_mine_ref,
        ga_theirs_ref,
        sum_ref,
        sum_up_ref,
        up_w,
        down_w,
        out_w,
        slope,
        sems,
    ) = rest[24:]
    step = pl.program_id(0)
    xz, my, mc = me_ref[0], me_ref[1], me_ref[2]
    xor = lax.bitwise_xor

    def copies():
        for dc in range(2):
            for dx in range(2):
                for dy in range(2):
                    i = dc * 4 + dx * 2 + dy
                    f = xor(my, dy) * 2 + xor(mc, dc)
                    for dz in range(4):
                        at = xor(xz, dx * 4 + dz)
                        fr = at // 2
                        pos = xor(fr % 2, mc) * 4 + xor(fr // 2, my) * 2 + at % 2
                        j = i * 4 + dz
                        yield pltpu.make_async_copy(out_p[i].at[dz], out_w.at[f, pos], sems.at[0, j])
                        yield pltpu.make_async_copy(up_p[i].at[dz], up_w.at[f, at], sems.at[1, j])
                        yield pltpu.make_async_copy(down_p[i].at[dz], down_w.at[at, f], sems.at[2, j])

    @pl.when(step == 0)
    def _():
        for copy in copies():
            copy.start()
        for copy in copies():
            copy.wait()
        sum_ref[...] = jnp.zeros_like(sum_ref)
        sum_up_ref[...] = jnp.zeros_like(sum_up_ref)

    mine, theirs = mine_ref[...], theirs_ref[...]
    mixed = join_columns(
        [
            dot(mine, out_w[f, 0:4].reshape(384, 256)) + dot(theirs, out_w[f, 4:8].reshape(384, 256))
            for f in range(4)
        ]
    )
    gain, last_gain = vec_ref[1:2], vec_ref[4:5]
    z1, r1 = center(x_ref[...].astype(f32) + (mixed + vec_ref[0:1]))
    normed = z1 * gain + vec_ref[2:3]
    low = normed.astype(bf16)
    nl_ref[...] = low
    branch = vec_ref[3:4] + normed
    for f in range(4):
        pre = dot(low, up_w[f].reshape(D, 768)) + upb_ref[f : f + 1]
        cdf = 0.5 + 0.5 * lax.erf(pre * (1.0 / math.sqrt(2.0)))
        act = (pre * cdf).astype(bf16)
        act_ref[:, f * 768 : f * 768 + 768] = act
        slope[f] = cdf + pre * jnp.exp(-0.5 * pre * pre) * (1.0 / math.sqrt(2.0 * math.pi))
        branch += dot(act[:, :384], down_w[2 * f].reshape(D, 384), NT)
        branch += dot(act[:, 384:], down_w[2 * f + 1].reshape(D, 384), NT)
    z2, r2 = center(branch)
    y_ref[...] = (z2 * last_gain + vec_ref[5:6]).astype(bf16)

    top = g_ref[...].astype(f32)
    grad_second = norm_back(top, z2, r2, last_gain)
    gb = grad_second.astype(bf16)
    gb_ref[...] = gb
    grad_normed = grad_second
    for f in range(4):
        ga = jnp.concatenate(
            [dot(gb, down_w[2 * f].reshape(D, 384)), dot(gb, down_w[2 * f + 1].reshape(D, 384))], axis=1
        )
        gp = (ga * slope[f]).astype(bf16)
        gp_ref[:, f * 768 : f * 768 + 768] = gp
        sum_up_ref[f : f + 1] += jnp.sum(gp.astype(f32), axis=0, keepdims=True)
        grad_normed += dot(gp, up_w[f].reshape(D, 768), NT)
    grad_first = norm_back(grad_normed, z1, r1, gain)
    gf_ref[...] = grad_first
    gm = grad_first.astype(bf16)
    gm32 = gm.astype(f32)
    parts = [p.astype(bf16) for p in part_columns(gm32)]
    gm_ref[...] = jnp.concatenate(parts, axis=1)
    ga = sum(dot(parts[f], out_w[f].reshape(D, 256), NT) for f in range(4))
    ga_mine_ref[...] = ga[:, :384].astype(bf16)
    ga_theirs_ref[...] = ga[:, 384:].astype(bf16)

    def total(i, value):
        sum_ref[i : i + 1] += jnp.sum(value, axis=0, keepdims=True)

    total(0, gm32)
    total(1, grad_normed * z1)
    total(2, grad_normed)
    total(3, gb.astype(f32))
    total(4, top * z2)
    total(5, top)


def middle(me, x, mine, theirs, g, vec, upb, up_p, down_p, out_p, block=256):
    rows = x.shape[0]

    def spec(width):
        return pl.BlockSpec((block, width), lambda i, m: (i, 0))

    def full(shape):
        return pl.BlockSpec(shape, lambda i, m: (0, 0))

    wide = [(D, bf16), (D, bf16), (FF, bf16), (D, bf16), (FF, bf16), (1024, bf16), (D, f32)]
    wide += [(384, bf16), (384, bf16)]
    return pl.pallas_call(
        middle_kernel,
        grid_spec=pltpu.PrefetchScalarGridSpec(
            num_scalar_prefetch=1,
            grid=(rows // block,),
            in_specs=[spec(D), spec(384), spec(384), spec(D), full((8, D)), full((4, D))] + [ANY] * 24,
            out_specs=[spec(w) for w, _ in wide] + [full((8, D)), full((4, D))],
            scratch_shapes=[
                pltpu.VMEM((4, 8, 96, 768), bf16),
                pltpu.VMEM((8, 4, 192, 384), bf16),
                pltpu.VMEM((4, 8, 96, 256), bf16),
                pltpu.VMEM((4, block, 768), f32),
                pltpu.SemaphoreType.DMA((3, 32)),
            ],
        ),
        out_shape=[jax.ShapeDtypeStruct((rows, w), t) for w, t in wide]
        + [jax.ShapeDtypeStruct((8, D), f32), jax.ShapeDtypeStruct((4, D), f32)],
        compiler_params=params(),
        cost_estimate=pl.CostEstimate(
            flops=rows * (D * D + 2 * D * FF) * 8, bytes_accessed=50 * 2**20, transcendentals=rows * FF
        ),
        name="middle",
    )(me, x, mine, theirs, g, vec, upb, *up_p, *down_p, *out_p)


def grad_up_kernel(me_ref, low_ref, gp_ref, o_ref, held):
    held[...] = dot(low_ref[...], gp_ref[...], TN).astype(bf16).reshape(8, 96, 768)
    for rel in range(8):
        o_ref[0, rel] = held[lax.bitwise_xor(me_ref[0], rel)]


def grad_up(me, low, gp, dc):
    rows = low.shape[0]
    return pl.pallas_call(
        grad_up_kernel,
        grid_spec=pltpu.PrefetchScalarGridSpec(
            num_scalar_prefetch=1,
            grid=(2,),
            in_specs=[
                pl.BlockSpec((rows, D), lambda i, m: (0, 0)),
                pl.BlockSpec(
                    (rows, D),
                    lambda i, m: (0, lax.bitwise_xor(m[1], i) * 2 + lax.bitwise_xor(m[2], dc)),
                ),
            ],
            out_specs=pl.BlockSpec((1, 8, 96, 768), lambda i, m: (i, 0, 0, 0)),
            scratch_shapes=[pltpu.VMEM((8, 96, 768), bf16)],
        ),
        out_shape=jax.ShapeDtypeStruct((2, 8, 96, 768), bf16),
        compiler_params=params(),
        cost_estimate=pl.CostEstimate(flops=rows * D * FF, bytes_accessed=8 * 2**20, transcendentals=0),
        name="grad_up",
    )(me, low, gp).reshape(2, 2, 4, 96, 768)


def grad_down_kernel(me_ref, gb_ref, act_ref, keep_ref, send_ref, held):
    held[...] = dot(gb_ref[...], act_ref[...], TN).astype(bf16).reshape(4, 192, 384)
    my, mc = me_ref[1], me_ref[2]
    for dy in range(2):
        y2 = lax.bitwise_xor(my, dy) * 2
        keep_ref[0, dy, 0] = held[y2 + mc]
        send_ref[0, dy, 0] = held[y2 + 1 - mc]


def grad_down(me, gb, act):
    rows = gb.shape[0]
    out = pl.BlockSpec((1, 2, 1, 192, 384), lambda i, m: (i // 4, 0, i % 4, 0, 0))
    return pl.pallas_call(
        grad_down_kernel,
        grid_spec=pltpu.PrefetchScalarGridSpec(
            num_scalar_prefetch=1,
            grid=(8,),
            in_specs=[
                pl.BlockSpec((rows, D), lambda i, m: (0, 0)),
                pl.BlockSpec((rows, 384), lambda i, m: (0, lax.bitwise_xor(m[0], i))),
            ],
            out_specs=[out] * 2,
            scratch_shapes=[pltpu.VMEM((4, 192, 384), bf16)],
        ),
        out_shape=[jax.ShapeDtypeStruct((2, 2, 4, 192, 384), bf16)] * 2,
        compiler_params=params(),
        cost_estimate=pl.CostEstimate(flops=rows * D * FF * 2, bytes_accessed=13 * 2**20, transcendentals=0),
        name="grad_down",
    )(me, gb, act)


def grad_out_kernel(me_ref, mine_ref, theirs_ref, gm_ref, keep_ref, send_ref, held):
    xz, my, mc = me_ref[0], me_ref[1], me_ref[2]
    for f in range(4):
        gm = gm_ref[:, f * 256 : f * 256 + 256]
        held[f, 0:4] = dot(mine_ref[...], gm, TN).astype(bf16).reshape(4, 96, 256)
        held[f, 4:8] = dot(theirs_ref[...], gm, TN).astype(bf16).reshape(4, 96, 256)
    for dy in range(2):
        y2 = lax.bitwise_xor(my, dy) * 2
        for rel in range(8):
            at = lax.bitwise_xor(xz, rel)
            fr = at // 2
            pos = lax.bitwise_xor(fr % 2, mc) * 4 + lax.bitwise_xor(fr // 2, my) * 2 + at % 2
            keep_ref[rel // 4, dy, rel % 4] = held[y2 + mc, pos]
            send_ref[rel // 4, dy, rel % 4] = held[y2 + 1 - mc, pos]


def grad_out(me, mine, theirs, gm):
    rows = gm.shape[0]
    return pl.pallas_call(
        grad_out_kernel,
        in_specs=[pl.BlockSpec(memory_space=pltpu.SMEM)] + [pl.BlockSpec(memory_space=pltpu.VMEM)] * 3,
        out_specs=[pl.BlockSpec(memory_space=pltpu.VMEM)] * 2,
        out_shape=[jax.ShapeDtypeStruct((2, 2, 4, 96, 256), bf16)] * 2,
        scratch_shapes=[pltpu.VMEM((4, 8, 96, 256), bf16)],
        compiler_params=params(),
        cost_estimate=pl.CostEstimate(flops=rows * D * D * 2, bytes_accessed=6 * 2**20, transcendentals=0),
        name="grad_out",
    )(me, mine, theirs, gm)


def grad_in_kernel(me_ref, x_ref, dq_ref, dk_ref, dv_ref, vec_ref, near_ref, far_ref, held):
    xz = me_ref[0]
    lane = lane_of((D, 128))
    for kind, ref in enumerate((dq_ref, dk_ref, dv_ref)):
        for dy, part in enumerate(part_columns(dot(x_ref[...], ref[...], TN))):
            if kind == 0:
                extra = vec_ref[...].reshape(D, 128)
                part = jnp.concatenate([part[:, :128], jnp.where(lane < 64, part[:, 128:], extra)], axis=1)
            held[dy] = part.astype(bf16).reshape(8, 96, 256)
        for rel in range(8):
            at = lax.bitwise_xor(xz, rel)
            near_ref[rel // 4, rel % 4, kind] = held[0, at]
            far_ref[rel // 4, rel % 4, kind] = held[1, at]


def grad_in(me, x, dq, dk, dv, vec):
    span = x.shape[0]
    return pl.pallas_call(
        grad_in_kernel,
        in_specs=[pl.BlockSpec(memory_space=pltpu.SMEM)] + [pl.BlockSpec(memory_space=pltpu.VMEM)] * 5,
        out_specs=[pl.BlockSpec(memory_space=pltpu.VMEM)] * 2,
        out_shape=[jax.ShapeDtypeStruct((2, 4, 3, 96, 256), bf16)] * 2,
        scratch_shapes=[pltpu.VMEM((2, 8, 96, 256), bf16)],
        compiler_params=params(),
        cost_estimate=pl.CostEstimate(flops=span * D * 2304, bytes_accessed=11 * 2**20, transcendentals=0),
        name="grad_in",
    )(me, x, dq, dk, dv, vec)


def grad_token_kernel(dq_ref, dk_ref, dv_ref, w_ref, o_ref):
    total = dot(dq_ref[...], w_ref[:, :384], NT)
    total += dot(dk_ref[...], w_ref[:, 384:768], NT)
    total += dot(dv_ref[...], w_ref[:, 768:], NT)
    o_ref[...] = total.astype(o_ref.dtype)


def grad_token(dq, dk, dv, w, part, kind, block=256):
    count = dq.shape[0] // 2 // block
    rows = pl.BlockSpec((block, 384), lambda i: (i + part * count, 0))
    return pl.pallas_call(
        grad_token_kernel,
        grid=(count,),
        in_specs=[rows, rows, rows, pl.BlockSpec((D, 1152), lambda i: (0, 0))],
        out_specs=pl.BlockSpec((block, D), lambda i: (i, 0)),
        out_shape=jax.ShapeDtypeStruct((count * block, D), kind),
        compiler_params=params(),
        cost_estimate=pl.CostEstimate(
            flops=count * block * D * 2304, bytes_accessed=7 * 2**20, transcendentals=0
        ),
        name="grad_token",
    )(dq, dk, dv, w)


AXES = ("dp", "seq", "y", "c")
SWAP = [(0, 1), (1, 0)]


def piece_routes():
    first, second = [], []
    for z in range(4):
        for y in range(2):
            for c in range(2):
                source = (z * 2 + y) * 2 + c
                for micro in range(2):
                    target = ((2 * micro + c) * 2 + y) * 2 + z // 2
                    (first if micro == z % 2 else second).append((source, target))
    return first, second


def back(route):
    return [(target, source) for source, target in route]


def along(array, axis):
    return lax.ppermute(array, axis, SWAP)


def across(array, step):
    return lax.ppermute(array, "seq", [(i, i ^ step) for i in range(4)])


def add(*arrays):
    return sum(a.astype(f32) for a in arrays).astype(bf16)


def column_gather(shard):
    return jnp.stack([shard] + [across(shard, step) for step in (1, 2, 3)])


def plane_gather(shard, order):
    base = column_gather(shard)
    first = along(base, order[0])
    third, fourth = along(base, order[1]), along(first, order[1])
    if order[0] == "y":
        return [base, first, third, fourth]
    return [base, third, first, fourth]


def chip_gather(shard, order):
    pieces = plane_gather(shard, order)
    return pieces + [along(p, "c") for p in pieces]


def column_reduce(pieces):
    got = [across(pieces[step], step) for step in (1, 2, 3)]
    return sum(a.astype(f32) for a in [pieces[0]] + got)


def plane_reduce(near, far, order):
    got = along(far, order[0])
    away = along(add(near[1], got[1]), order[1])
    return column_reduce([add(near[0][i], got[0][i], away[i]) for i in range(4)])


def chip_reduce(keep, send, order):
    got = along(send, "c")
    return plane_reduce(add(keep[0], got[0]), add(keep[1], got[1]), order)


def local_pairs(
    tokens,
    lengths,
    in_weight,
    in_bias,
    out_weight,
    out_bias,
    mid_gain,
    mid_shift,
    up_weight,
    up_bias,
    down_weight,
    down_bias,
    last_gain,
    last_shift,
    grad_output,
):
    rows = tokens.shape[2]
    z = lax.axis_index("seq")
    y = lax.axis_index("y")
    c = lax.axis_index("c")
    xz = lax.axis_index("dp") * 4 + z
    me = jnp.stack([xz, y, c]).astype(jnp.int32)
    odd = z % 2
    route_a, route_b = piece_routes()
    where_to = ("seq", "y", "c")

    def spread(array):
        own = lax.dynamic_index_in_dim(array[:, 0], odd, 0, keepdims=False)
        other = lax.dynamic_index_in_dim(array[:, 0], 1 - odd, 0, keepdims=False)
        return jnp.concatenate(
            [lax.ppermute(own, where_to, route_a), lax.ppermute(other, where_to, route_b)], axis=0
        )

    def collect(array):
        own = lax.ppermute(array[:rows], where_to, back(route_a))
        other = lax.ppermute(array[rows:], where_to, back(route_b))
        return jnp.stack(
            [jnp.where(odd == 0, own, other), jnp.where(odd == 0, other, own)], axis=0
        )[:, None]

    vectors = (in_bias, out_bias, mid_gain, mid_shift, up_bias, down_bias, last_gain, last_shift)
    packed = jnp.pad(jnp.concatenate(vectors).reshape(18, HEAD), ((0, 78), (0, 0)))
    shard = in_weight.reshape(96, 3, 192).transpose(1, 0, 2)
    extra = jnp.stack([packed, jnp.zeros_like(packed), jnp.zeros_like(packed)])
    in_pieces = plane_gather(jnp.concatenate([shard, extra], axis=2), ("y", "dp"))
    x = spread(tokens)
    out_pieces = chip_gather(jnp.pad(out_weight, ((0, 0), (0, 64))), ("dp", "y"))
    up_pieces = chip_gather(up_weight, ("y", "dp"))
    down_pieces = chip_gather(down_weight.T, ("dp", "y"))
    g_top = spread(grad_output)

    near = jnp.stack([in_pieces[0][:, 0, :18, 192:], in_pieces[2][:, 0, :18, 192:]])
    near = near.reshape(8, 1152)
    index = jnp.arange(8, dtype=jnp.int32) ^ xz
    known = jnp.dot(
        (index[:, None] == jnp.arange(8, dtype=jnp.int32)[None, :]).astype(bf16),
        near,
        preferred_element_type=f32,
    )
    whole = []
    at = 0
    for v in vectors:
        whole.append(known[:, at : at + v.shape[0]].reshape(-1))
        at += v.shape[0]
    in_vector, out_vector, mid_scale, mid_offset, up_vector, down_vector, last_scale, last_offset = whole
    zero = jnp.zeros_like(out_vector)
    vec = jnp.stack(
        [out_vector, mid_scale, mid_offset, down_vector, last_scale, last_offset, zero, zero]
    )

    micro = z // 2
    group = (lax.axis_index("dp") * 2 + y) * 2 + odd
    length = lengths[micro, group]
    iota = jnp.arange(rows, dtype=jnp.int32)

    def places(core):
        return [(2 * core + micro) * rows + iota, (2 * core + 1 - micro) * rows + iota]

    place = jnp.concatenate(places(c) + places(1 - c))
    mask = jnp.where(place < length, 0.0, -1e30).astype(bf16)
    half = 2 * rows
    lane = jnp.arange(128, dtype=jnp.int32)[None, :]
    aux = jnp.where(
        lane == 64, mask[:, None], jnp.where((lane > 64) & (lane < 68), -1.0, 0.0).astype(bf16)
    )

    def by_distance(array):
        return jnp.where(y == 0, array, array[::-1])

    x_full = jnp.concatenate([x, along(x, "c")], axis=0)
    bias = lax.dynamic_index_in_dim(in_vector.reshape(2, 2, 3, 2, HEAD), c, 1, keepdims=False)
    bias = by_distance(bias).reshape(6, 2, HEAD)
    b_head = jnp.concatenate(
        [bias[:, 0], jnp.zeros_like(bias[:, 0]), bias[:, 1], jnp.zeros_like(bias[:, 0])], axis=1
    )[:, None]
    q, k, v, w_kind = project(me, x_full, b_head, aux, in_pieces)
    attended, q = attend(q, k, v)
    mine = attended[:half]
    theirs = along(attended[half:], "c")
    (result, low, act, gb, gp, gm, grad_first, g_own, g_other, sums, sums_up) = middle(
        me, x, mine, theirs, g_top, vec, up_vector.reshape(4, D), up_pieces, down_pieces, out_pieces
    )
    result = collect(result)

    g_other = along(g_other, "c")
    up_send = grad_up(me, low, gp, 1)
    up_keep = grad_up(me, low, gp, 0)
    down_keep, down_send = grad_down(me, gb, act)
    out_keep, out_send = grad_out(me, mine, theirs, gm)
    dq, dk, dv = attend_back(q, k, v, attended, jnp.concatenate([g_own, g_other], axis=0))
    out_up = chip_reduce(up_keep, up_send, ("y", "dp"))
    out_down = chip_reduce(down_keep, down_send, ("dp", "y")).T
    out_out = chip_reduce(out_keep, out_send, ("dp", "y"))[:, :192]

    core = (jnp.arange(2) == c).astype(f32)
    own_bias = jnp.stack([row_sum(dq).reshape(2, 3, HEAD), row_sum(dv).reshape(2, 3, HEAD)], axis=2)
    vec_in = (by_distance(own_bias)[:, None] * core[None, :, None, None, None]).reshape(-1)
    grads = (vec_in, sums[0], sums[1], sums[2], sums_up, sums[3], sums[4], sums[5])
    packed = jnp.concatenate([g.reshape(8, -1) for g in grads], axis=1).reshape(8, 18, HEAD)
    packed = jnp.pad(packed, ((0, 0), (0, 78), (64, 0)))
    in_near, in_far = grad_in(me, x_full, dq, dk, dv, packed)
    partial = along(grad_token(dq, dk, dv, w_kind, 1, bf16), "c")
    got = plane_reduce(in_near, in_far, ("y", "dp"))
    out_in = got[:, :, :192].reshape(3, 96, 3, HEAD).transpose(1, 2, 0, 3).reshape(96, 576)
    total = got[0, :18, 192:].reshape(1152)
    total = total + along(total, "c")
    own = grad_token(dq, dk, dv, w_kind, 0, f32)
    grad_tokens = collect((grad_first + own + partial.astype(f32)).astype(bf16)).astype(f32)
    sums = []
    at = 0
    for vector in vectors:
        sums.append(total[at : at + vector.shape[0]])
        at += vector.shape[0]
    return (
        result,
        grad_tokens,
        out_in,
        sums[0],
        out_out,
        sums[1],
        sums[2],
        sums[3],
        out_up,
        sums[4],
        out_down,
        sums[5],
        sums[6],
        sums[7],
    )


def specs(fsdp):
    data = P(None, ("dp",) + fsdp, "seq", None)
    matrix = P(("dp", "seq"), fsdp)
    vector = P(("dp", "seq"))
    ins = (data, P(), matrix, vector, matrix, vector, vector, vector, matrix, vector, matrix, vector)
    ins += (vector, vector, data)
    outs = (data, data, matrix, vector, matrix, vector, vector, vector, matrix, vector, matrix)
    outs += (vector, vector, vector)
    return ins, outs


def solution(mesh):
    if tuple(mesh.shape[name] for name in ("dp", "seq", "fsdp")) == (2, 4, 4):
        mesh = jax.sharding.Mesh(mesh.devices.reshape(2, 4, 2, 2), AXES)
        body, (ins, outs) = local_pairs, specs(("y", "c"))
    else:
        body, (ins, outs) = local, specs(("fsdp",))
    return jax.shard_map(body, mesh=mesh, in_specs=ins, out_specs=outs, check_vma=False)
```
